256 devices in a mesh: dp: 32 (over y_lo, z, core), mp: 8 (over x, y_hi).
Axes of the slice: x: 4, y: 4 (y_hi: 2, y_lo: 2; y = y_hi * 2 + y_lo), z: 8, core: 2. Of those that a mesh axis runs over, the one named last changes fastest.
Arguments:
- tokens: bfloat16 [8192, 3072], P('dp', 'mp'), may hold values from -6 to 6
- w_query: bfloat16 [3072, 3072], P('dp', 'mp'), may hold values from -0.109375 to 0.109375
- w_key: bfloat16 [3072, 3072], P('dp', 'mp'), may hold values from -0.109375 to 0.109375
- w_value: bfloat16 [3072, 3072], P('dp', 'mp'), may hold values from -0.109375 to 0.109375
- w_out: bfloat16 [3072, 3072], P('mp', 'dp'), may hold values from -0.21875 to 0.21875
- cotangent: bfloat16 [8192, 3072], P('dp', 'mp'), may hold values from -6 to 6
Outputs:
- output: bfloat16 [8192, 3072], P('dp', 'mp')
- input_grad: bfloat16 [8192, 3072], P('dp', 'mp')
- query_weight_grad: bfloat16 [3072, 3072], P('dp', 'mp')
- key_weight_grad: bfloat16 [3072, 3072], P('dp', 'mp')
- value_weight_grad: bfloat16 [3072, 3072], P('dp', 'mp')
- out_weight_grad: bfloat16 [3072, 3072], P('mp', 'dp')
The draws below stay inside these ranges and needn't reach their ends.
All inputs are finite; a program needn't handle non-finite values.
Results may differ from the reference program's by a relative error of at most 0.035.
Values may be sent and summed in bfloat16 or wider, within the bound.
No kernel may reach another device: no remote copies, remote signals or barrier semaphores. Data moves between devices by JAX's collectives and lax.ppermute only.
A program may use at most 128 MiB of HBM per device.

```python
import math
import jax
import jax.numpy as jnp
from jax import lax

D = 3072
HEADS = 24
HEAD_DIM = 128
IMG_TOK = 64
TOK_DEV = 256
TOKENS = 8192
HD = 3072
N_DP = 32


def draw_tokens(key, part):
    key = jax.random.fold_in(key, 11)
    key_columns, key_rows, key_entries = jax.random.split(key, 3)
    column_scale = jnp.power(10.0, jax.random.uniform(key_columns, (D,), jnp.float32, -0.5, 0.5))
    column_scale = column_scale * (0.5 + jnp.arange(D, dtype=jnp.float32) / D)
    row_scale = jnp.power(10.0, jax.random.uniform(key_rows, (TOKENS, 1), jnp.float32, -0.5, 0.5))
    entries = jnp.clip(jax.random.normal(key_entries, (TOKENS, D), jnp.float32), -4.0, 4.0)
    return (0.1 * entries * row_scale * column_scale).astype(jnp.bfloat16)


def strengthened(drawn, rng, source, target, parts, factor):
    def block_of(dim):
        return (jnp.arange(drawn.shape[dim]) // (drawn.shape[dim] // parts)).reshape((-1,) + (1,) * (drawn.ndim - 1 - dim))

    one_side = jax.random.permutation(rng, parts)[block_of(target)]
    other_side = (block_of(target) + parts // 2) % parts
    return jnp.where((block_of(source) == one_side) | (block_of(source) == other_side), factor * drawn, drawn)


def level_of(key, shape, pieces, smallest, top_value):
    def one(dim, blocks):
        heights = jax.random.uniform(jax.random.fold_in(jax.random.fold_in(key, 6), dim), (blocks,), jnp.float32, smallest / len(pieces), top_value / len(pieces))
        return jnp.repeat(jnp.exp(heights), shape[dim] // blocks).reshape((-1,) + (1,) * (len(shape) - dim - 1))

    loudness = one(*pieces[0])
    for cut in pieces[1:]:
        loudness = loudness * one(*cut)
    return loudness


def normal_values(stream_key, extent, scale, limit, cuts=(), kind=jnp.bfloat16):
    values = scale * jax.random.normal(stream_key, extent, jnp.float32)
    if cuts:
        values = values * level_of(stream_key, extent, cuts, -0.22, 0.18)
    return jnp.clip(values, -limit, limit).astype(kind)


def noise_with(rng, extent, scale, reach, shards, heavy, kind=jnp.bfloat16):
    result = scale * jax.random.normal(rng, extent, jnp.float32)
    if shards:
        result = result * level_of(rng, extent, shards, -0.22, 0.18)
    return jnp.clip(strengthened(result, jax.random.fold_in(rng, 3), *heavy), -reach, reach).astype(kind)


def setup_inputs(seed: int = 0) -> dict:
    arg_keys = jax.random.split(jax.random.key(seed), 7)
    tokens = draw_tokens(jax.random.fold_in(arg_keys[6], 71), 0)
    w_query = normal_values(arg_keys[1], (D, HD), D ** -0.5, 0.109375, ((0, 32), (1, 8)))
    w_key = normal_values(arg_keys[2], (D, HD), D ** -0.5, 0.109375, ((0, 32), (1, 8)))
    w_value = normal_values(arg_keys[3], (D, HD), D ** -0.5, 0.109375, ((0, 32), (1, 8)))
    w_out = normal_values(arg_keys[4], (HD, D), (HD // 4) ** -0.5, 0.21875, ((0, 8), (1, 32)))
    cotangent = noise_with(arg_keys[5], (TOKENS, D), 1.0, 6.0, ((0, 32), (1, 8)), (0, 1, 32, 2.75))
    return dict(tokens=tokens, w_query=w_query, w_key=w_key, w_value=w_value, w_out=w_out, cotangent=cotangent)


def layer_norm(matrix):
    values = matrix.astype(jnp.float32)
    center = values - lax.optimization_barrier(jnp.mean(values, axis=-1, keepdims=True))
    spread = lax.rsqrt(lax.optimization_barrier(jnp.mean(center * center, axis=-1, keepdims=True)) + 1e-06)
    return (center * spread, spread)

def attend(query_raw, key_raw, value_raw):
    token_count, head_count, head_width = query_raw.shape
    image_shape = (token_count // IMG_TOK, IMG_TOK, head_count, head_width)
    query = layer_norm(query_raw)[0].astype(jnp.bfloat16).reshape(image_shape)
    keys = layer_norm(key_raw)[0].astype(jnp.bfloat16).reshape(image_shape)
    value = value_raw.astype(jnp.bfloat16).reshape(image_shape)
    scores = jnp.einsum('bqhd,bkhd->bhqk', query.astype(jnp.float32), keys.astype(jnp.float32)) / math.sqrt(head_width)
    weights = jnp.exp(scores)
    probability = (weights / lax.optimization_barrier(jnp.sum(weights, axis=-1, keepdims=True))).astype(jnp.bfloat16)
    attended = jnp.einsum('bhqk,bkhd->bqhd', probability.astype(jnp.float32), value.astype(jnp.float32))
    return attended.astype(jnp.bfloat16).reshape(token_count, head_count * head_width)

def reference(tokens, w_query, w_key, w_value, w_out, cotangent):
    normed, spread = layer_norm(tokens)
    hidden = normed.astype(jnp.bfloat16)
    split_shape = (TOKENS, HEADS, HEAD_DIM)
    query_raw = jnp.dot(hidden, w_query, preferred_element_type=jnp.float32).reshape(split_shape)
    key_raw = jnp.dot(hidden, w_key, preferred_element_type=jnp.float32).reshape(split_shape)
    value_raw = jnp.dot(hidden, w_value, preferred_element_type=jnp.float32).reshape(split_shape)
    attended, backward = jax.vjp(attend, query_raw, key_raw, value_raw)
    branch = jnp.dot(attended, w_out, preferred_element_type=jnp.float32)
    output = (tokens.astype(jnp.float32) + branch).astype(jnp.bfloat16)
    attended_grad = jnp.dot(cotangent, w_out.T, preferred_element_type=jnp.float32).astype(jnp.bfloat16)
    query_grad, key_grad, value_grad = backward(attended_grad)
    query_grad = query_grad.reshape(TOKENS, HD).astype(jnp.bfloat16)
    key_grad = key_grad.reshape(TOKENS, HD).astype(jnp.bfloat16)
    value_grad = value_grad.reshape(TOKENS, HD).astype(jnp.bfloat16)
    hidden_grad = jnp.dot(query_grad, w_query.T, preferred_element_type=jnp.float32)
    hidden_grad = hidden_grad + jnp.dot(key_grad, w_key.T, preferred_element_type=jnp.float32)
    hidden_grad = hidden_grad + jnp.dot(value_grad, w_value.T, preferred_element_type=jnp.float32)
    first_mean = lax.optimization_barrier(jnp.mean(hidden_grad, axis=-1, keepdims=True))
    second_mean = lax.optimization_barrier(jnp.mean(hidden_grad * normed, axis=-1, keepdims=True))
    input_grad = spread * (hidden_grad - first_mean - normed * second_mean) + cotangent.astype(jnp.float32)
    input_grad = input_grad.astype(jnp.bfloat16)
    stacked = jnp.concatenate([query_grad, key_grad, value_grad], axis=1)
    grad_scale = 1.0 / math.sqrt(TOKENS)

    def accumulate(running, position):
        first_row = (position * TOK_DEV).astype(jnp.int32)
        hidden_rows = lax.dynamic_slice_in_dim(hidden, first_row, TOK_DEV, 0)
        stacked_rows = lax.dynamic_slice_in_dim(stacked, first_row, TOK_DEV, 0)
        cotangent_rows = lax.dynamic_slice_in_dim(cotangent, first_row, TOK_DEV, 0)
        attended_rows = lax.dynamic_slice_in_dim(attended, first_row, TOK_DEV, 0)
        partial_value = jnp.concatenate([jnp.dot(hidden_rows.T, stacked_rows, preferred_element_type=jnp.float32), jnp.dot(cotangent_rows.T, attended_rows, preferred_element_type=jnp.float32)], axis=1) * grad_scale
        rounded = lax.optimization_barrier(partial_value.astype(jnp.bfloat16))
        return (running + rounded.astype(jnp.float32), None)
    weight_sum, _ = lax.scan(accumulate, jnp.zeros((D, 4 * HD), jnp.float32), jnp.arange(N_DP, dtype=jnp.int32))
    query_weight_grad = weight_sum[:, :HD].astype(jnp.bfloat16)
    key_weight_grad = weight_sum[:, HD:2 * HD].astype(jnp.bfloat16)
    value_weight_grad = weight_sum[:, 2 * HD:3 * HD].astype(jnp.bfloat16)
    out_weight_grad = weight_sum[:, 3 * HD:].T.astype(jnp.bfloat16)
    return (output, input_grad, query_weight_grad, key_weight_grad, value_weight_grad, out_weight_grad)
```

```python
import math

import jax
import jax.numpy as jnp
from jax import lax
from jax.experimental import pallas as pl
from jax.experimental.pallas import tpu as pltpu
from jax.sharding import Mesh
from jax.sharding import PartitionSpec as P

HEAD_DIM = 128
IMG_TOK = 64
EPS = 1e-06
BF16 = jnp.bfloat16
F32 = jnp.float32
N_YL, N_Z, N_C, N_X, N_YH = 2, 8, 2, 4, 2


def shift(value, axis, step, size):
    return lax.ppermute(value, axis, [(i, (i + step) % size) for i in range(size)])


def dot(a, b, contract):
    return lax.dot_general(a, b, ((contract[:1], contract[1:]), ((), ())), preferred_element_type=F32)


def norm_parts(raw):
    center = raw - jnp.mean(raw, axis=-1, keepdims=True)
    spread = lax.rsqrt(jnp.mean(center * center, axis=-1, keepdims=True) + EPS)
    return center * spread, spread


def norm_back(grad, normed, spread):
    first = jnp.mean(grad, axis=-1, keepdims=True)
    second = jnp.mean(grad * normed, axis=-1, keepdims=True)
    return spread * (grad - first - normed * second)


def attention_kernel(mine_ref, other_ref, grads_ref):
    rows, cols = mine_ref.shape
    width = cols // 4
    image = lax.broadcasted_iota(jnp.int32, (rows, rows), 0) // IMG_TOK
    same = image == lax.broadcasted_iota(jnp.int32, (rows, rows), 1) // IMG_TOK
    scale = 1.0 / math.sqrt(HEAD_DIM)
    for head in range(width // HEAD_DIM):
        spans = [pl.ds(part * width + head * HEAD_DIM, HEAD_DIM) for part in range(4)]
        query_raw, key_raw, value_raw, attended_grad = (
            mine_ref[:, span] + other_ref[:, span] for span in spans
        )
        query_normed, query_spread = norm_parts(query_raw)
        key_normed, key_spread = norm_parts(key_raw)
        query, key, value = query_normed.astype(BF16), key_normed.astype(BF16), value_raw.astype(BF16)
        attended_grad = attended_grad.astype(BF16)
        weights = jnp.where(same, jnp.exp(dot(query, key, (1, 1)) * scale), 0.0)
        exact = weights / jnp.sum(weights, axis=-1, keepdims=True)
        probability = exact.astype(BF16)
        attended = dot(probability, value, (1, 0))
        value_grad = dot(probability, attended_grad, (0, 0))
        probability_grad = dot(attended_grad, value, (1, 1)).astype(BF16).astype(F32)
        inner = jnp.sum(probability_grad * exact, axis=-1, keepdims=True)
        scores_grad = (exact * (probability_grad - inner) * scale).astype(BF16)
        query_grad = dot(scores_grad, key, (1, 0)).astype(BF16).astype(F32)
        key_grad = dot(scores_grad, query, (0, 0)).astype(BF16).astype(F32)
        grads_ref[:, spans[0]] = norm_back(query_grad, query_normed, query_spread).astype(BF16)
        grads_ref[:, spans[1]] = norm_back(key_grad, key_normed, key_spread).astype(BF16)
        grads_ref[:, spans[2]] = value_grad.astype(BF16)
        grads_ref[:, spans[3]] = attended.astype(BF16)


def attention(mine, other):
    whole = pl.BlockSpec(memory_space=pltpu.VMEM)
    return pl.pallas_call(
        attention_kernel,
        out_shape=jax.ShapeDtypeStruct(mine.shape, BF16),
        in_specs=[whole, whole],
        out_specs=whole,
        compiler_params=pltpu.CompilerParams(vmem_limit_bytes=24 * 1024 * 1024),
    )(mine, other)


def gather_weights(packed, z_place):
    rows, cols = packed.shape
    half = rows // 2
    yl_place = lax.axis_index("yl")
    other = shift(packed, "yl", 1, N_YL)
    pair = jnp.where(yl_place == 0, jnp.stack([packed, other]), jnp.stack([other, packed]))
    full = jnp.zeros((N_YL, N_Z, rows, cols), BF16)

    def place(full, piece, step, row):
        return lax.dynamic_update_slice(full, piece[:, None], (0, (z_place + step) % N_Z, row, 0))

    full = place(full, pair, 0, 0)
    up = down = pair
    for step in range(1, N_Z // 2):
        up, down = shift(up, "z", 1, N_Z), shift(down, "z", -1, N_Z)
        full = place(full, up, -step, 0)
        full = place(full, down, step, 0)
    up, down = shift(up[:, :half], "z", 1, N_Z), shift(down[:, half:], "z", -1, N_Z)
    full = place(full, up, N_Z // 2, 0)
    full = place(full, down, N_Z // 2, half)
    return full.reshape(N_YL * N_Z * rows, cols)


def scatter_weights(grads, z_place):
    cols = grads.shape[-1]
    half = cols // 2

    def block(step):
        return lax.dynamic_index_in_dim(grads, (z_place + step) % N_Z, 1, keepdims=False)

    far = block(N_Z // 2)
    down = shift(far[..., :half], "z", -1, N_Z)
    up = shift(far[..., half:], "z", 1, N_Z)
    nothing = jnp.zeros_like(down)
    down = jnp.concatenate([down, nothing], axis=-1)
    up = jnp.concatenate([nothing, up], axis=-1)
    for step in range(N_Z // 2 - 1, 0, -1):
        down = shift((block(-step).astype(F32) + down.astype(F32)).astype(BF16), "z", -1, N_Z)
        up = shift((block(step).astype(F32) + up.astype(F32)).astype(BF16), "z", 1, N_Z)
    total = block(0).astype(F32) + down.astype(F32) + up.astype(F32)
    yl_place = lax.axis_index("yl")
    sent = lax.dynamic_index_in_dim(total, 1 - yl_place, 0, keepdims=False).astype(BF16)
    kept = lax.dynamic_index_in_dim(total, yl_place, 0, keepdims=False)
    return kept + shift(sent, "yl", 1, N_YL).astype(F32)


def gather_features(block):
    rows, cols = block.shape
    x_place, yh_place = lax.axis_index("x"), lax.axis_index("yh")
    other = shift(block, "yh", 1, N_YH)
    pair = jnp.where(yh_place == 0, jnp.stack([block, other]), jnp.stack([other, block]))
    full = jnp.zeros((N_X, N_YH, rows, cols), BF16)

    def place(full, piece, step, row):
        return lax.dynamic_update_slice(full, piece[None], ((x_place + step) % N_X, 0, row, 0))

    full = place(full, pair, 0, 0)
    up, down = shift(pair, "x", 1, N_X), shift(pair, "x", -1, N_X)
    full = place(full, up, -1, 0)
    full = place(full, down, 1, 0)
    half = rows // 2
    up, down = shift(up[:, :half], "x", 1, N_X), shift(down[:, half:], "x", -1, N_X)
    full = place(full, up, 2, 0)
    full = place(full, down, 2, half)
    return full.reshape(N_X * N_YH * rows, cols)


def scatter_features(parts):
    x_place, yh_place = lax.axis_index("x"), lax.axis_index("yh")
    parts = parts.astype(BF16)

    def block(step):
        return lax.dynamic_index_in_dim(parts, (x_place + step) % N_X, 0, keepdims=False)

    arrived = [shift(block(step), "x", step, N_X) for step in range(1, N_X)]
    total = block(0).astype(F32)
    for piece in arrived:
        total = total + piece.astype(F32)
    sent = lax.dynamic_index_in_dim(total, 1 - yh_place, 0, keepdims=False).astype(BF16)
    kept = lax.dynamic_index_in_dim(total, yh_place, 0, keepdims=False)
    return kept + shift(sent, "yh", 1, N_YH).astype(F32)


def sum_features(value):
    value = value + shift(value, "yh", 1, N_YH)
    return value + sum(shift(value, "x", step, N_X) for step in range(1, N_X))


def shards(tokens, w_query, w_key, w_value, w_out, cotangent):
    z_place, core = lax.axis_index("z"), lax.axis_index("c")
    row_count, local_cols = tokens.shape
    width = w_query.shape[1]
    feat = w_query.shape[0]
    packed = jnp.concatenate([w_query, w_key, w_value, w_out.T], axis=1)
    weights = gather_weights(packed, z_place)

    tokens_t, cotangent_t = tokens.T, cotangent.T
    both = jnp.concatenate([tokens_t, cotangent_t], axis=1).reshape(
        local_cols // (N_C * feat), N_C, feat, 2 * row_count
    )
    kept = lax.dynamic_index_in_dim(both, core, 1, keepdims=False)
    sent = lax.dynamic_index_in_dim(both, 1 - core, 1, keepdims=False)
    other = shift(sent, "c", 1, N_C)
    block = jnp.concatenate(
        [kept[..., :row_count], other[..., :row_count], kept[..., row_count:], other[..., row_count:]],
        axis=-1,
    ).reshape(local_cols // N_C, 4 * row_count)
    features = gather_features(block)
    half_rows = features.shape[0]
    tokens_c = features[:, : 2 * row_count].astype(F32)
    cotangent_c = features[:, 2 * row_count :]

    half_mean = jnp.mean(tokens_c, axis=0)
    half_square = jnp.sum((tokens_c - half_mean) ** 2, axis=0)
    half_stats = jnp.stack([half_mean, half_square])
    other_stats = shift(jnp.roll(half_stats, row_count, axis=1), "c", 1, N_C)
    mean = 0.5 * (half_stats[0] + other_stats[0])
    gap = half_stats[0] - other_stats[0]
    square = half_stats[1] + other_stats[1] + (0.5 * half_rows) * gap * gap
    spread = lax.rsqrt(square / (2 * half_rows) + EPS)
    normed = (tokens_c - mean) * spread
    hidden = normed.astype(BF16)

    def project(columns):
        return jnp.concatenate(
            [
                dot(hidden[:, columns], weights[:, : 3 * width], (0, 0)),
                dot(cotangent_c[:, columns], weights[:, 3 * width :], (0, 0)),
            ],
            axis=1,
        )

    from_other = shift(project(slice(row_count, None)), "c", 1, N_C)
    grads_mine = attention(project(slice(0, row_count)), from_other)
    grads = jnp.concatenate([grads_mine, shift(grads_mine, "c", 1, N_C)], axis=0)

    grad_scale = 1.0 / math.sqrt(row_count * N_YL * N_Z * N_C)
    weight_parts = (
        jnp.concatenate(
            [
                dot(hidden, grads[:, : 3 * width], (1, 0)),
                dot(cotangent_c, grads[:, 3 * width :], (1, 0)),
            ],
            axis=1,
        )
        * grad_scale
    ).astype(BF16)
    weight_sums = scatter_weights(weight_parts.reshape(N_YL, N_Z, feat, 4 * width), z_place).astype(BF16)

    hidden_part = dot(weights[:, : 3 * width], grads[:, : 3 * width], (1, 1))
    branch_part = dot(weights[:, 3 * width :], grads[:, 3 * width :], (1, 1))
    sums = jnp.stack([jnp.sum(hidden_part, axis=0), jnp.sum(hidden_part * normed, axis=0)])
    sums = sums[:, :row_count] + shift(sums[:, row_count:], "c", 1, N_C)
    means = sum_features(sums) / (2 * half_rows)

    back = scatter_features(
        jnp.concatenate([hidden_part, branch_part], axis=1).reshape(
            N_X, N_YH, local_cols // N_C, 4 * row_count
        )
    ).reshape(local_cols // (N_C * feat), feat, 2, 2, row_count)
    mine, other = back[:, :, :, 0], shift(back[:, :, :, 1], "c", 1, N_C)
    whole = jnp.where(core == 0, jnp.stack([mine, other], 1), jnp.stack([other, mine], 1)).reshape(
        local_cols, 2, row_count
    )
    own_normed = (tokens_t.astype(F32) - mean[:row_count]) * spread[:row_count]
    input_grad = spread[:row_count] * (whole[:, 0] - means[0] - own_normed * means[1])
    input_grad = (input_grad + cotangent_t.astype(F32)).astype(BF16).T
    output = (whole[:, 1] + tokens_t.astype(F32)).astype(BF16).T
    return (
        output,
        input_grad,
        weight_sums[:, :width],
        weight_sums[:, width : 2 * width],
        weight_sums[:, 2 * width : 3 * width],
        weight_sums[:, 3 * width :].T,
    )


def solution(mesh):
    split = Mesh(
        mesh.devices.reshape(N_YL, N_Z, N_C, N_X, N_YH), ("yl", "z", "c", "x", "yh")
    )
    dp, mp = ("yl", "z", "c"), ("x", "yh")
    placed = (P(dp, mp),) * 4 + (P(mp, dp), P(dp, mp))
    return jax.shard_map(
        shards,
        mesh=split,
        in_specs=placed,
        out_specs=(P(dp, mp),) * 5 + (P(mp, dp),),
        check_vma=False,
    )
```

```python
import math

import jax
import jax.numpy as jnp
from jax import lax
from jax.experimental import pallas as pl
from jax.experimental.pallas import tpu as pltpu
from jax.sharding import Mesh
from jax.sharding import PartitionSpec as P

HEAD_DIM = 128
IMG_TOK = 64
EPS = 1e-06
BF16 = jnp.bfloat16
F32 = jnp.float32
N_YL, N_Z, N_C, N_X, N_YH = 2, 8, 2, 4, 2


def shift(value, axis, step, size):
    return lax.ppermute(value, axis, [(i, (i + step) % size) for i in range(size)])


def dot(a, b, contract):
    return lax.dot_general(a, b, ((contract[:1], contract[1:]), ((), ())), preferred_element_type=F32)


def norm_parts(raw):
    center = raw - jnp.mean(raw, axis=-1, keepdims=True)
    spread = lax.rsqrt(jnp.mean(center * center, axis=-1, keepdims=True) + EPS)
    return center * spread, spread


def norm_back(grad, normed, spread):
    first = jnp.mean(grad, axis=-1, keepdims=True)
    second = jnp.mean(grad * normed, axis=-1, keepdims=True)
    return spread * (grad - first - normed * second)


def attention_kernel(mine_ref, other_ref, grads_ref):
    rows, cols = mine_ref.shape
    width = cols // 4
    image = lax.broadcasted_iota(jnp.int32, (rows, rows), 0) // IMG_TOK
    same = image == lax.broadcasted_iota(jnp.int32, (rows, rows), 1) // IMG_TOK
    scale = 1.0 / math.sqrt(HEAD_DIM)
    for head in range(width // HEAD_DIM):
        spans = [pl.ds(part * width + head * HEAD_DIM, HEAD_DIM) for part in range(4)]
        query_raw, key_raw, value_raw, attended_grad = (
            mine_ref[:, span] + other_ref[:, span] for span in spans
        )
        query_normed, query_spread = norm_parts(query_raw)
        key_normed, key_spread = norm_parts(key_raw)
        query, key, value = query_normed.astype(BF16), key_normed.astype(BF16), value_raw.astype(BF16)
        attended_grad = attended_grad.astype(BF16)
        weights = jnp.where(same, jnp.exp(dot(query, key, (1, 1)) * scale), 0.0)
        exact = weights / jnp.sum(weights, axis=-1, keepdims=True)
        probability = exact.astype(BF16)
        attended = dot(probability, value, (1, 0))
        value_grad = dot(probability, attended_grad, (0, 0))
        probability_grad = dot(attended_grad, value, (1, 1)).astype(BF16).astype(F32)
        inner = jnp.sum(probability_grad * exact, axis=-1, keepdims=True)
        scores_grad = (exact * (probability_grad - inner) * scale).astype(BF16)
        query_grad = dot(scores_grad, key, (1, 0)).astype(BF16).astype(F32)
        key_grad = dot(scores_grad, query, (0, 0)).astype(BF16).astype(F32)
        grads_ref[:, spans[0]] = norm_back(query_grad, query_normed, query_spread).astype(BF16)
        grads_ref[:, spans[1]] = norm_back(key_grad, key_normed, key_spread).astype(BF16)
        grads_ref[:, spans[2]] = value_grad.astype(BF16)
        grads_ref[:, spans[3]] = attended.astype(BF16)


def attention(mine, other):
    whole = pl.BlockSpec(memory_space=pltpu.VMEM)
    return pl.pallas_call(
        attention_kernel,
        out_shape=jax.ShapeDtypeStruct(mine.shape, BF16),
        in_specs=[whole, whole],
        out_specs=whole,
        compiler_params=pltpu.CompilerParams(vmem_limit_bytes=24 * 1024 * 1024),
    )(mine, other)


def weight_kernel(hidden_ref, cotangent_ref, grads_ref, out_ref, *, split, scale):
    first = dot(hidden_ref[...], grads_ref[:, :split], (1, 0))
    out_ref[:, :split] = (first * scale).astype(BF16)
    second = dot(cotangent_ref[...], grads_ref[:, split:], (1, 0))
    out_ref[:, split:] = (second * scale).astype(BF16)


def weight_grads(hidden, cotangent, grads, split, scale):
    rows, depth = hidden.shape
    cols = grads.shape[1]
    tile = rows // 4
    return pl.pallas_call(
        lambda *refs: weight_kernel(*refs, split=split, scale=scale),
        out_shape=jax.ShapeDtypeStruct((rows, cols), BF16),
        grid=(rows // tile,),
        in_specs=[
            pl.BlockSpec((tile, depth), lambda i: (i, 0)),
            pl.BlockSpec((tile, depth), lambda i: (i, 0)),
            pl.BlockSpec((depth, cols), lambda i: (0, 0)),
        ],
        out_specs=pl.BlockSpec((tile, cols), lambda i: (i, 0)),
        compiler_params=pltpu.CompilerParams(vmem_limit_bytes=24 * 1024 * 1024),
    )(hidden, cotangent, grads)


def gather_weights(packed, z_place):
    rows, cols = packed.shape
    half = rows // 2
    yl_place = lax.axis_index("yl")
    other = shift(packed, "yl", 1, N_YL)
    pair = jnp.where(yl_place == 0, jnp.stack([packed, other]), jnp.stack([other, packed]))
    full = jnp.zeros((N_YL, N_Z, rows, cols), BF16)

    def place(full, piece, step, row):
        return lax.dynamic_update_slice(full, piece[:, None], (0, (z_place + step) % N_Z, row, 0))

    full = place(full, pair, 0, 0)
    up = down = pair
    for step in range(1, N_Z // 2):
        up, down = shift(up, "z", 1, N_Z), shift(down, "z", -1, N_Z)
        full = place(full, up, -step, 0)
        full = place(full, down, step, 0)
    up, down = shift(up[:, :half], "z", 1, N_Z), shift(down[:, half:], "z", -1, N_Z)
    full = place(full, up, N_Z // 2, 0)
    full = place(full, down, N_Z // 2, half)
    return full.reshape(N_YL * N_Z * rows, cols)


def gather_features(block):
    rows, cols = block.shape
    x_place, yh_place = lax.axis_index("x"), lax.axis_index("yh")
    other = shift(block, "yh", 1, N_YH)
    pair = jnp.where(yh_place == 0, jnp.stack([block, other]), jnp.stack([other, block]))
    full = jnp.zeros((N_X, N_YH, rows, cols), BF16)

    def place(full, piece, step, row):
        return lax.dynamic_update_slice(full, piece[None], ((x_place + step) % N_X, 0, row, 0))

    full = place(full, pair, 0, 0)
    up, down = shift(pair, "x", 1, N_X), shift(pair, "x", -1, N_X)
    full = place(full, up, -1, 0)
    full = place(full, down, 1, 0)
    half = rows // 2
    up, down = shift(up[:, :half], "x", 1, N_X), shift(down[:, half:], "x", -1, N_X)
    full = place(full, up, 2, 0)
    full = place(full, down, 2, half)
    return full.reshape(N_X * N_YH * rows, cols)


def swap(value, axis, bit, size):
    return lax.ppermute(value, axis, [(i, i ^ bit) for i in range(size)])


def add(a, b):
    return (a.astype(F32) + b.astype(F32)).astype(BF16)


def reduce_back(grads, parts, sums):
    tie = lambda *values: lax.optimization_barrier(values)
    yl_place, z_place = lax.axis_index("yl"), lax.axis_index("z")
    x_place, yh_place = lax.axis_index("x"), lax.axis_index("yh")

    def block(step):
        return lax.dynamic_index_in_dim(grads, (z_place + step) % N_Z, 1, keepdims=False)

    def piece(step):
        return lax.dynamic_index_in_dim(parts, (x_place + step) % N_X, 0, keepdims=False)

    half = grads.shape[-1] // 2
    far = block(4)
    down, up = shift(far[..., :half], "z", -1, N_Z), shift(far[..., half:], "z", 1, N_Z)
    parts, sums = parts(), sums()
    down, up, parts, sums = tie(down, up, parts, sums)

    nothing = jnp.zeros_like(down)
    down = jnp.concatenate([down, nothing], axis=-1)
    up = jnp.concatenate([nothing, up], axis=-1)
    down, up = shift(add(block(-3), down), "z", -1, N_Z), shift(add(block(3), up), "z", 1, N_Z)
    side = parts.shape[-1] // 2
    far = piece(2)
    left, right = shift(far[..., :side], "x", -1, N_X), shift(far[..., side:], "x", 1, N_X)
    tokens = sums.shape[1] // 2
    sums = sums[:, :tokens] + shift(sums[:, tokens:], "c", 1, N_C)
    down, up, left, right, sums = tie(down, up, left, right, sums)

    down, up = shift(add(block(-2), down), "z", -1, N_Z), shift(add(block(2), up), "z", 1, N_Z)
    nothing = jnp.zeros_like(left)
    left = jnp.concatenate([left, nothing], axis=-1)
    right = jnp.concatenate([nothing, right], axis=-1)
    left, right = shift(add(piece(-1), left), "x", -1, N_X), shift(add(piece(1), right), "x", 1, N_X)
    sums = sums + shift(sums, "yh", 1, N_YH)
    down, up, left, right, sums = tie(down, up, left, right, sums)

    down, up = shift(add(block(-1), down), "z", -1, N_Z), shift(add(block(1), up), "z", 1, N_Z)
    total = piece(0).astype(F32) + left.astype(F32) + right.astype(F32)
    sent = lax.dynamic_index_in_dim(total, 1 - yh_place, 0, keepdims=False).astype(BF16)
    kept = lax.dynamic_index_in_dim(total, yh_place, 0, keepdims=False)
    other = shift(sent, "yh", 1, N_YH)
    sums = sums + swap(sums, "x", 1, N_X)
    down, up, other, sums = tie(down, up, other, sums)

    features = kept + other.astype(F32)
    total = block(0).astype(F32) + down.astype(F32) + up.astype(F32)
    sent = lax.dynamic_index_in_dim(total, 1 - yl_place, 0, keepdims=False).astype(BF16)
    kept = lax.dynamic_index_in_dim(total, yl_place, 0, keepdims=False)
    sums = sums + swap(sums, "x", 2, N_X)
    return kept + shift(sent, "yl", 1, N_YL).astype(F32), features, sums


def shards(tokens, w_query, w_key, w_value, w_out, cotangent):
    z_place, core = lax.axis_index("z"), lax.axis_index("c")
    row_count, local_cols = tokens.shape
    width = w_query.shape[1]
    feat = w_query.shape[0]
    packed = jnp.concatenate([w_query, w_key, w_value, w_out.T], axis=1)
    weights = gather_weights(packed, z_place)

    tokens_t, cotangent_t = tokens.T, cotangent.T
    both = jnp.concatenate([tokens_t, cotangent_t], axis=1).reshape(
        local_cols // (N_C * feat), N_C, feat, 2 * row_count
    )
    kept = lax.dynamic_index_in_dim(both, core, 1, keepdims=False)
    sent = lax.dynamic_index_in_dim(both, 1 - core, 1, keepdims=False)
    other = shift(sent, "c", 1, N_C)
    block = jnp.concatenate(
        [kept[..., :row_count], other[..., :row_count], kept[..., row_count:], other[..., row_count:]],
        axis=-1,
    ).reshape(local_cols // N_C, 4 * row_count)
    features = gather_features(block)
    half_rows = features.shape[0]
    tokens_c = features[:, : 2 * row_count].astype(F32)
    cotangent_c = features[:, 2 * row_count :]

    half_mean = jnp.mean(tokens_c, axis=0)
    half_square = jnp.sum((tokens_c - half_mean) ** 2, axis=0)
    half_stats = jnp.stack([half_mean, half_square])
    other_stats = shift(jnp.roll(half_stats, row_count, axis=1), "c", 1, N_C)
    mean = 0.5 * (half_stats[0] + other_stats[0])
    gap = half_stats[0] - other_stats[0]
    square = half_stats[1] + other_stats[1] + (0.5 * half_rows) * gap * gap
    spread = lax.rsqrt(square / (2 * half_rows) + EPS)
    normed = (tokens_c - mean) * spread
    hidden = normed.astype(BF16)

    def project(columns):
        return jnp.concatenate(
            [
                dot(hidden[:, columns], weights[:, : 3 * width], (0, 0)),
                dot(cotangent_c[:, columns], weights[:, 3 * width :], (0, 0)),
            ],
            axis=1,
        )

    from_other = shift(project(slice(row_count, None)), "c", 1, N_C)
    grads_mine = attention(project(slice(0, row_count)), from_other)
    grads = jnp.concatenate([grads_mine, shift(grads_mine, "c", 1, N_C)], axis=0)

    grad_scale = 1.0 / math.sqrt(row_count * N_YL * N_Z * N_C)
    weight_parts = weight_grads(hidden, cotangent_c, grads, 3 * width, grad_scale)
    hidden_part = dot(weights[:, : 3 * width], grads[:, : 3 * width], (1, 1))
    branch_part = dot(weights[:, 3 * width :], grads[:, 3 * width :], (1, 1))

    def parts():
        return jnp.concatenate([hidden_part.astype(BF16), branch_part.astype(BF16)], axis=1).reshape(
            N_X, N_YH, local_cols // N_C, 4 * row_count
        )

    def sums():
        return jnp.stack([jnp.sum(hidden_part, axis=0), jnp.sum(hidden_part * normed, axis=0)])

    weight_sums, back, means = reduce_back(
        weight_parts.reshape(N_YL, N_Z, feat, 4 * width), parts, sums
    )
    weight_sums = weight_sums.astype(BF16)
    means = means / (2 * half_rows)
    back = back.reshape(local_cols // (N_C * feat), feat, 2, 2, row_count)
    mine, other = back[:, :, :, 0], shift(back[:, :, :, 1], "c", 1, N_C)
    whole = jnp.where(core == 0, jnp.stack([mine, other], 1), jnp.stack([other, mine], 1)).reshape(
        local_cols, 2, row_count
    )
    own_normed = (tokens_t.astype(F32) - mean[:row_count]) * spread[:row_count]
    input_grad = spread[:row_count] * (whole[:, 0] - means[0] - own_normed * means[1])
    input_grad = (input_grad + cotangent_t.astype(F32)).astype(BF16).T
    output = (whole[:, 1] + tokens_t.astype(F32)).astype(BF16).T
    return (
        output,
        input_grad,
        weight_sums[:, :width],
        weight_sums[:, width : 2 * width],
        weight_sums[:, 2 * width : 3 * width],
        weight_sums[:, 3 * width :].T,
    )


def solution(mesh):
    split = Mesh(
        mesh.devices.reshape(N_YL, N_Z, N_C, N_X, N_YH), ("yl", "z", "c", "x", "yh")
    )
    dp, mp = ("yl", "z", "c"), ("x", "yh")
    placed = (P(dp, mp),) * 4 + (P(mp, dp), P(dp, mp))
    return jax.shard_map(
        shards,
        mesh=split,
        in_specs=placed,
        out_specs=(P(dp, mp),) * 5 + (P(mp, dp),),
        check_vma=False,
    )
```

```python
import math

import jax
import jax.numpy as jnp
from jax import lax
from jax.experimental import pallas as pl
from jax.experimental.pallas import tpu as pltpu
from jax.sharding import Mesh
from jax.sharding import PartitionSpec as P

HEAD_DIM = 128
IMG_TOK = 64
EPS = 1e-06
BF16 = jnp.bfloat16
F32 = jnp.float32
N_YL, N_Z, N_C, N_X, N_YH = 2, 8, 2, 4, 2
HOLD_FLOPS, HOLD_BYTES = 12_000_000_000, 40_000_000


def shift(value, axis, step, size):
    return lax.ppermute(value, axis, [(i, (i + step) % size) for i in range(size)])


def dot(a, b, contract):
    return lax.dot_general(a, b, ((contract[:1], contract[1:]), ((), ())), preferred_element_type=F32)


def norm_parts(raw):
    center = raw - jnp.mean(raw, axis=-1, keepdims=True)
    spread = lax.rsqrt(jnp.mean(center * center, axis=-1, keepdims=True) + EPS)
    return center * spread, spread


def norm_back(grad, normed, spread):
    first = jnp.mean(grad, axis=-1, keepdims=True)
    second = jnp.mean(grad * normed, axis=-1, keepdims=True)
    return spread * (grad - first - normed * second)


def attention_kernel(mine_ref, other_ref, grads_ref):
    rows, cols = mine_ref.shape
    width = cols // 4
    image = lax.broadcasted_iota(jnp.int32, (rows, rows), 0) // IMG_TOK
    same = image == lax.broadcasted_iota(jnp.int32, (rows, rows), 1) // IMG_TOK
    scale = 1.0 / math.sqrt(HEAD_DIM)
    for head in range(width // HEAD_DIM):
        spans = [pl.ds(part * width + head * HEAD_DIM, HEAD_DIM) for part in range(4)]
        query_raw, key_raw, value_raw, attended_grad = (
            mine_ref[:, span] + other_ref[:, span] for span in spans
        )
        query_normed, query_spread = norm_parts(query_raw)
        key_normed, key_spread = norm_parts(key_raw)
        query, key, value = query_normed.astype(BF16), key_normed.astype(BF16), value_raw.astype(BF16)
        attended_grad = attended_grad.astype(BF16)
        weights = jnp.where(same, jnp.exp(dot(query, key, (1, 1)) * scale), 0.0)
        exact = weights / jnp.sum(weights, axis=-1, keepdims=True)
        probability = exact.astype(BF16)
        attended = dot(probability, value, (1, 0))
        value_grad = dot(probability, attended_grad, (0, 0))
        probability_grad = dot(attended_grad, value, (1, 1)).astype(BF16).astype(F32)
        inner = jnp.sum(probability_grad * exact, axis=-1, keepdims=True)
        scores_grad = (exact * (probability_grad - inner) * scale).astype(BF16)
        query_grad = dot(scores_grad, key, (1, 0)).astype(BF16).astype(F32)
        key_grad = dot(scores_grad, query, (0, 0)).astype(BF16).astype(F32)
        grads_ref[:, spans[0]] = norm_back(query_grad, query_normed, query_spread).astype(BF16)
        grads_ref[:, spans[1]] = norm_back(key_grad, key_normed, key_spread).astype(BF16)
        grads_ref[:, spans[2]] = value_grad.astype(BF16)
        grads_ref[:, spans[3]] = attended.astype(BF16)


def attention(mine, other):
    whole = pl.BlockSpec(memory_space=pltpu.VMEM)
    return pl.pallas_call(
        attention_kernel,
        out_shape=jax.ShapeDtypeStruct(mine.shape, BF16),
        in_specs=[whole, whole],
        out_specs=whole,
        compiler_params=pltpu.CompilerParams(vmem_limit_bytes=14 * 1024 * 1024),
    )(mine, other)


def weight_kernel(hidden_ref, cotangent_ref, grads_ref, out_ref, *, split, scale):
    first = dot(hidden_ref[...], grads_ref[:, :split], (1, 0))
    out_ref[:, :split] = (first * scale).astype(BF16)
    second = dot(cotangent_ref[...], grads_ref[:, split:], (1, 0))
    out_ref[:, split:] = (second * scale).astype(BF16)


def weight_grads(hidden, cotangent, grads, split, scale):
    rows, depth = hidden.shape
    cols = grads.shape[1]
    tile = rows // 4
    return pl.pallas_call(
        lambda *refs: weight_kernel(*refs, split=split, scale=scale),
        out_shape=jax.ShapeDtypeStruct((rows, cols), BF16),
        grid=(rows // tile,),
        in_specs=[
            pl.BlockSpec((tile, depth), lambda i: (i, 0)),
            pl.BlockSpec((tile, depth), lambda i: (i, 0)),
            pl.BlockSpec((depth, cols), lambda i: (0, 0)),
        ],
        out_specs=pl.BlockSpec((tile, cols), lambda i: (i, 0)),
        compiler_params=pltpu.CompilerParams(vmem_limit_bytes=14 * 1024 * 1024),
    )(hidden, cotangent, grads)


def tie(*values):
    return lax.optimization_barrier(values)


def hold_kernel(*refs):
    count = (len(refs) - 1) // 2
    for source, target in zip(refs[1 : 1 + count], refs[1 + count :]):
        target[...] = source[...]


def after(main, *held):
    tile = (16, HEAD_DIM)
    corners = [main[: tile[0], : tile[1]]]
    corners += [value[(0,) * (value.ndim - 2)][: tile[0], : tile[1]] for value in held]
    whole = pl.BlockSpec(memory_space=pltpu.VMEM)
    passed = pl.pallas_call(
        hold_kernel,
        out_shape=[jax.ShapeDtypeStruct(tile, value.dtype) for value in held],
        in_specs=[whole] * len(corners),
        out_specs=[whole] * len(held),
        compiler_params=pltpu.CompilerParams(vmem_limit_bytes=1024 * 1024),
        cost_estimate=pl.CostEstimate(flops=HOLD_FLOPS, bytes_accessed=HOLD_BYTES, transcendentals=0),
    )(*corners)
    return tuple(
        lax.dynamic_update_slice(value, tile.reshape((1,) * (value.ndim - 2) + tile.shape), (0,) * value.ndim)
        for value, tile in zip(held, passed)
    )


def rows(*pieces):
    return jnp.concatenate(pieces, axis=0)


def ordered(place, mine, other):
    return jnp.where(place == 0, rows(mine, other), rows(other, mine))


def gather_all(packed, block):
    yl_place, z_place = lax.axis_index("yl"), lax.axis_index("z")
    x_place, yh_place = lax.axis_index("x"), lax.axis_index("yh")
    n, cols = packed.shape
    side = cols // 2
    m, wide = block.shape
    wide //= 2
    weights = jnp.zeros((N_YL, N_Z, n, cols), BF16)
    features = jnp.zeros((N_X, N_YH * m, 2 * wide), BF16)

    def put_pair(weights, piece, step, row=0):
        piece = piece.reshape(N_YL, 1, -1, side)
        return lax.dynamic_update_slice(weights, piece, (0, (z_place + step) % N_Z, row, 0))

    def put_one(weights, piece, step, swapped, row=0):
        place = 1 - yl_place if swapped else yl_place
        return lax.dynamic_update_slice(
            weights, piece[None, None], (place, (z_place + step) % N_Z, row, side)
        )

    def put_x(features, piece, step, row=0):
        return lax.dynamic_update_slice(features, piece[None], ((x_place + step) % N_X, row, 0))

    first, second = packed[:, :side], packed[:, side:]
    other = shift(first, "yl", 1, N_YL)
    up, down = shift(second, "z", 1, N_Z), shift(second, "z", -1, N_Z)
    block_other = shift(block, "yh", 1, N_YH)

    pair = ordered(yl_place, first, other)
    weights = put_pair(weights, pair, 0)
    weights = put_one(weights, second, 0, False)
    weights = put_one(weights, up, -1, False)
    weights = put_one(weights, down, 1, False)
    ones = [up, down]
    up, down = tie(rows(pair, up), rows(pair, down))
    second, block = after(up, second, ordered(yh_place, block, block_other))
    up, down = shift(up, "z", 1, N_Z), shift(down, "z", -1, N_Z)
    other = shift(second, "yl", 1, N_YL)
    right, left = shift(block, "x", 1, N_X), shift(block, "x", -1, N_X)

    weights = put_pair(weights, up[: 2 * n], -1)
    weights = put_pair(weights, down[: 2 * n], 1)
    weights = put_one(weights, up[2 * n :], -2, False)
    weights = put_one(weights, down[2 * n :], 2, False)
    ones += [up[2 * n :], down[2 * n :]]
    up, down = tie(up, down)
    (others,) = after(up, rows(*ones))
    up, down = shift(up, "z", 1, N_Z), shift(down, "z", -1, N_Z)
    others = shift(others, "yl", 1, N_YL)

    weights = put_one(weights, other, 0, True)
    weights = put_pair(weights, up[: 2 * n], -2)
    weights = put_pair(weights, down[: 2 * n], 2)
    weights = put_one(weights, up[2 * n :], -3, False)
    weights = put_one(weights, down[2 * n :], 3, False)
    half = 2 * n + n // 2
    last = rows(up[2 * n :], down[2 * n :])
    up, down = tie(up[:half], rows(down[: 2 * n], down[half:]))
    last, far_right, far_left = after(up, last, right[:m], left[m:])
    up, down = shift(up, "z", 1, N_Z), shift(down, "z", -1, N_Z)
    last = shift(last, "yl", 1, N_YL)
    features = put_x(put_x(put_x(features, block, 0), right, -1), left, 1)
    right, left = shift(far_right, "x", 1, N_X), shift(far_left, "x", -1, N_X)

    for place, step in enumerate((-1, 1, -2, 2)):
        weights = put_one(weights, others[place * n : (place + 1) * n], step, True)
    weights = put_pair(weights, up[: 2 * n], -3)
    weights = put_pair(weights, down[: 2 * n], 3)
    other = rows(up[2 * n :], down[2 * n :])
    weights = put_one(weights, other, 4, False)
    upper = up[: 2 * n].reshape(N_YL, n, side)[:, : n // 2].reshape(n, side)
    lower = down[: 2 * n].reshape(N_YL, n, side)[:, n // 2 :].reshape(n, side)
    up, down = tie(upper, lower)
    (other,) = after(up, other)
    up, down = shift(up, "z", 1, N_Z), shift(down, "z", -1, N_Z)
    other = shift(other, "yl", 1, N_YL)

    weights = put_one(weights, last[:n], -3, True)
    weights = put_one(weights, last[n:], 3, True)
    weights = put_one(weights, other, 4, True)
    weights = put_pair(put_pair(weights, up, 4), down, 4, n // 2)
    features = put_x(put_x(features, right, 2), left, 2, m)
    features = features.reshape(N_X * N_YH * m, 2 * wide)
    return weights.reshape(N_YL * N_Z * n, cols), features[:, :wide], features[:, wide:]


def high_low(total):
    high = lax.reduce_precision(total, 8, 7)
    return jnp.concatenate([high.astype(BF16), (total - high).astype(BF16)], axis=-2)


def with_sums(values, sums):
    return jnp.concatenate([values.astype(BF16), high_low(sums)], axis=-2)


def apart(packed):
    sums = packed[..., -16:, :].astype(F32)
    return packed[..., :-16, :].astype(F32), sums[..., :8, :] + sums[..., 8:, :]


def fold_apart(*packed):
    values, sums = zip(*(apart(p) for p in packed))
    return sum(values), sum(sums)


def add(a, b):
    return (a.astype(F32) + b.astype(F32)).astype(BF16)


def reduce_back(grads, parts):
    yl_place, z_place = lax.axis_index("yl"), lax.axis_index("z")
    x_place, yh_place = lax.axis_index("x"), lax.axis_index("yh")
    _, _, n, cols = grads.shape
    side = cols // 2

    def pair(step):
        found = lax.dynamic_slice(grads, (0, (z_place + step) % N_Z, 0, 0), (N_YL, 1, n, side))
        return found.reshape(N_YL * n, side)

    def one(step, swapped):
        place = 1 - yl_place if swapped else yl_place
        found = lax.dynamic_slice(grads, (place, (z_place + step) % N_Z, 0, side), (1, 1, n, side))
        return found.reshape(n, side)

    def piece(values, step):
        return lax.dynamic_index_in_dim(values, (x_place + step) % N_X, 0, keepdims=False)

    def flat(values):
        return values.reshape(-1, values.shape[-1])

    def pick(values, place):
        return lax.dynamic_index_in_dim(values, place, 0, keepdims=False)

    def fold(mine, *arrived):
        return sum((a.astype(F32) for a in arrived), mine.astype(F32))

    def send_z(down, up):
        return shift(down, "z", -1, N_Z), shift(up, "z", 1, N_Z)

    far = pair(4)
    down, up = send_z(far[:n], far[n:])
    far_other = shift(one(4, True), "yl", 1, N_YL)
    other = shift(rows(one(-3, True), one(3, True)), "yl", 1, N_YL)
    packed = parts()
    down, up, far_other, packed = tie(down, up, far_other, packed)

    far = fold(one(4, False), far_other).astype(BF16)
    below, above = pair(-3), pair(3)
    down, up = tie(
        rows(add(below[:n], down), below[n:], far[: n // 2]),
        rows(above[:n], add(above[n:], up), far[n // 2 :]),
    )
    far_left, far_right = piece(packed, 2)
    other_next, left, right = after(down, rows(one(-2, True), one(2, True)), far_left, far_right)
    down, up = send_z(down, up)
    other_next = shift(other_next, "yl", 1, N_YL)
    left, right = shift(left, "x", -1, N_X), shift(right, "x", 1, N_X)

    pad = jnp.zeros((n // 2, side), BF16)
    down, up = tie(
        rows(add(pair(-2), down[: 2 * n]), fold(one(-3, False), other[:n], rows(down[2 * n :], pad)).astype(BF16)),
        rows(add(pair(2), up[: 2 * n]), fold(one(3, False), other[n:], rows(pad, up[2 * n :])).astype(BF16)),
    )
    other = other_next
    mine_left, mine_right = piece(packed, -1), piece(packed, 1)
    other_next, left, right = after(
        down,
        rows(one(-1, True), one(1, True), one(0, True)),
        jnp.stack([with_sums(*fold_apart(mine_left[0], left)), mine_left[1]]),
        jnp.stack([mine_right[0], with_sums(*fold_apart(mine_right[1], right))]),
    )
    down, up = send_z(down, up)
    other_next = shift(other_next, "yl", 1, N_YL)
    left, right = shift(left, "x", -1, N_X), shift(right, "x", 1, N_X)

    down, up = tie(
        rows(add(pair(-1), down[: 2 * n]), fold(one(-2, False), other[:n], down[2 * n :]).astype(BF16)),
        rows(add(pair(1), up[: 2 * n]), fold(one(2, False), other[n:], up[2 * n :]).astype(BF16)),
    )
    other = other_next
    down, up = send_z(down, up)

    total = fold(pair(0), down[: 2 * n], up[: 2 * n]).reshape(N_YL, n, side)
    down, up = tie(
        fold(one(-1, False), other[:n], down[2 * n :]).astype(BF16),
        fold(one(1, False), other[n : 2 * n], up[2 * n :]).astype(BF16),
    )
    values, sums = fold_apart(piece(packed, 0), left, right)
    sent, back = after(
        down,
        pick(total, 1 - yl_place).astype(BF16),
        with_sums(pick(values, 1 - yh_place), pick(sums, 1 - yh_place)),
    )
    down, up = send_z(down, up)
    first = pick(total, yl_place) + shift(sent, "yl", 1, N_YL).astype(F32)
    other_values, other_sums = apart(shift(back, "yh", 1, N_YH))
    features = rows(pick(values, yh_place) + other_values, pick(sums, yh_place) + other_sums)
    second = fold(one(0, False), other[2 * n :], down, up)
    return jnp.concatenate([first, second], axis=1), features


def shards(tokens, w_query, w_key, w_value, w_out, cotangent):
    core = lax.axis_index("c")
    row_count, local_cols = tokens.shape
    width = w_query.shape[1]
    feat = w_query.shape[0]
    packed = jnp.concatenate([w_query, w_key, w_value, w_out.T], axis=1)
    tokens_t, cotangent_t = tokens.T, cotangent.T
    both = jnp.concatenate([tokens_t, cotangent_t], axis=1).reshape(
        local_cols // (N_C * feat), N_C, feat, 2 * row_count
    )
    kept = lax.dynamic_index_in_dim(both, core, 1, keepdims=False)
    sent = lax.dynamic_index_in_dim(both, 1 - core, 1, keepdims=False)
    other = shift(sent, "c", 1, N_C)
    other, packed = tie(other, packed)
    block = jnp.concatenate(
        [kept[..., :row_count], other[..., :row_count], kept[..., row_count:], other[..., row_count:]],
        axis=-1,
    ).reshape(local_cols // N_C, 4 * row_count)
    weights, tokens_c, cotangent_c = gather_all(packed, block)
    half_rows = tokens_c.shape[0]
    tokens_c = tokens_c.astype(F32)

    half_mean = jnp.mean(tokens_c, axis=0)
    half_square = jnp.sum((tokens_c - half_mean) ** 2, axis=0)
    half_stats = jnp.stack([half_mean, half_square])
    other_stats = shift(jnp.roll(half_stats, row_count, axis=1), "c", 1, N_C)
    mean = 0.5 * (half_stats[0] + other_stats[0])
    gap = half_stats[0] - other_stats[0]
    square = half_stats[1] + other_stats[1] + (0.5 * half_rows) * gap * gap
    spread = lax.rsqrt(square / (2 * half_rows) + EPS)
    normed = (tokens_c - mean) * spread
    hidden = normed.astype(BF16)

    def project(columns):
        return jnp.concatenate(
            [
                dot(hidden[:, columns], weights[:, : 3 * width], (0, 0)),
                dot(cotangent_c[:, columns], weights[:, 3 * width :], (0, 0)),
            ],
            axis=1,
        )

    from_other = shift(project(slice(row_count, None)), "c", 1, N_C)
    grads_mine = attention(project(slice(0, row_count)), from_other)
    grads = jnp.concatenate([grads_mine, shift(grads_mine, "c", 1, N_C)], axis=0)

    grad_scale = 1.0 / math.sqrt(row_count * N_YL * N_Z * N_C)
    weight_parts = weight_grads(hidden, cotangent_c, grads, 3 * width, grad_scale)
    hidden_part = dot(weights[:, : 3 * width], grads[:, : 3 * width], (1, 1))
    branch_part = dot(weights[:, 3 * width :], grads[:, 3 * width :], (1, 1))

    def parts():
        shape = (N_X, N_YH, local_cols // N_C, 2 * row_count)
        values = jnp.concatenate([hidden_part.reshape(shape), branch_part.reshape(shape)], axis=2)
        sums = jnp.stack([jnp.sum(hidden_part, axis=0), jnp.sum(hidden_part * normed, axis=0)])
        sums = jnp.broadcast_to(jnp.pad(sums, ((0, 6), (0, 0))), (N_X, N_YH, 8, 2 * row_count))
        return with_sums(values, sums)

    weight_sums, mine = reduce_back(weight_parts.reshape(N_YL, N_Z, feat, 4 * width), parts)
    weight_sums = weight_sums.astype(BF16)
    mine, other = mine[:, :row_count], shift(mine[:, row_count:], "c", 1, N_C)
    means = (mine[-8:-6] + other[-8:-6]) / (2 * half_rows)
    mine, other = (v[:local_cols].reshape(2, -1, 1, feat, row_count) for v in (mine, other))
    both = jnp.where(core == 0, jnp.concatenate([mine, other], 2), jnp.concatenate([other, mine], 2))
    hidden_sum, branch_sum = both.reshape(2, local_cols, row_count)
    own_normed = (tokens_t.astype(F32) - mean[:row_count]) * spread[:row_count]
    input_grad = spread[:row_count] * (hidden_sum - means[0] - own_normed * means[1])
    input_grad = (input_grad + cotangent_t.astype(F32)).astype(BF16).T
    output = (branch_sum + tokens_t.astype(F32)).astype(BF16).T
    return (
        output,
        input_grad,
        weight_sums[:, :width],
        weight_sums[:, width : 2 * width],
        weight_sums[:, 2 * width : 3 * width],
        weight_sums[:, 3 * width :].T,
    )


def solution(mesh):
    split = Mesh(
        mesh.devices.reshape(N_YL, N_Z, N_C, N_X, N_YH), ("yl", "z", "c", "x", "yh")
    )
    dp, mp = ("yl", "z", "c"), ("x", "yh")
    placed = (P(dp, mp),) * 4 + (P(mp, dp), P(dp, mp))
    return jax.shard_map(
        shards,
        mesh=split,
        in_specs=placed,
        out_specs=(P(dp, mp),) * 5 + (P(mp, dp),),
        check_vma=False,
    )
```

```python
import math

import jax
import jax.numpy as jnp
from jax import lax
from jax.experimental import pallas as pl
from jax.experimental.pallas import tpu as pltpu
from jax.sharding import Mesh
from jax.sharding import PartitionSpec as P

HEAD_DIM = 128
IMG_TOK = 64
EPS = 1e-06
BF16 = jnp.bfloat16
F32 = jnp.float32
N_YL, N_Z, N_C, N_X, N_YH = 2, 8, 2, 4, 2
HOLD_FLOPS, HOLD_BYTES = 12_000_000_000, 40_000_000


def shift(value, axis, step, size):
    return lax.ppermute(value, axis, [(i, (i + step) % size) for i in range(size)])


def dot(a, b, contract):
    return lax.dot_general(a, b, ((contract[:1], contract[1:]), ((), ())), preferred_element_type=F32)


def norm_parts(raw):
    center = raw - jnp.mean(raw, axis=-1, keepdims=True)
    spread = lax.rsqrt(jnp.mean(center * center, axis=-1, keepdims=True) + EPS)
    return center * spread, spread


def norm_back(grad, normed, spread):
    first = jnp.mean(grad, axis=-1, keepdims=True)
    second = jnp.mean(grad * normed, axis=-1, keepdims=True)
    return spread * (grad - first - normed * second)


def attention_kernel(mine_ref, other_ref, grads_ref):
    rows, cols = mine_ref.shape
    width = cols // 4
    image = lax.broadcasted_iota(jnp.int32, (rows, rows), 0) // IMG_TOK
    same = image == lax.broadcasted_iota(jnp.int32, (rows, rows), 1) // IMG_TOK
    scale = 1.0 / math.sqrt(HEAD_DIM)
    for head in range(width // HEAD_DIM):
        spans = [pl.ds(part * width + head * HEAD_DIM, HEAD_DIM) for part in range(4)]
        query_raw, key_raw, value_raw, attended_grad = (
            mine_ref[:, span] + other_ref[:, span] for span in spans
        )
        query_normed, query_spread = norm_parts(query_raw)
        key_normed, key_spread = norm_parts(key_raw)
        query, key, value = query_normed.astype(BF16), key_normed.astype(BF16), value_raw.astype(BF16)
        attended_grad = attended_grad.astype(BF16)
        weights = jnp.where(same, jnp.exp(dot(query, key, (1, 1)) * scale), 0.0)
        exact = weights / jnp.sum(weights, axis=-1, keepdims=True)
        probability = exact.astype(BF16)
        attended = dot(probability, value, (1, 0))
        value_grad = dot(probability, attended_grad, (0, 0))
        probability_grad = dot(attended_grad, value, (1, 1)).astype(BF16).astype(F32)
        inner = jnp.sum(probability_grad * exact, axis=-1, keepdims=True)
        scores_grad = (exact * (probability_grad - inner) * scale).astype(BF16)
        query_grad = dot(scores_grad, key, (1, 0)).astype(BF16).astype(F32)
        key_grad = dot(scores_grad, query, (0, 0)).astype(BF16).astype(F32)
        grads_ref[:, spans[0]] = norm_back(query_grad, query_normed, query_spread).astype(BF16)
        grads_ref[:, spans[1]] = norm_back(key_grad, key_normed, key_spread).astype(BF16)
        grads_ref[:, spans[2]] = value_grad.astype(BF16)
        grads_ref[:, spans[3]] = attended.astype(BF16)


def attention(mine, other):
    whole = pl.BlockSpec(memory_space=pltpu.VMEM)
    return pl.pallas_call(
        attention_kernel,
        out_shape=jax.ShapeDtypeStruct(mine.shape, BF16),
        in_specs=[whole, whole],
        out_specs=whole,
        compiler_params=pltpu.CompilerParams(vmem_limit_bytes=14 * 1024 * 1024),
    )(mine, other)


def weight_kernel(hidden_ref, cotangent_ref, grads_ref, out_ref, *, split, scale):
    first = dot(hidden_ref[...], grads_ref[:, :split], (1, 0))
    out_ref[:, :split] = (first * scale).astype(BF16)
    second = dot(cotangent_ref[...], grads_ref[:, split:], (1, 0))
    out_ref[:, split:] = (second * scale).astype(BF16)


def weight_grads(hidden, cotangent, grads, split, scale):
    rows, depth = hidden.shape
    cols = grads.shape[1]
    tile = rows // 4
    return pl.pallas_call(
        lambda *refs: weight_kernel(*refs, split=split, scale=scale),
        out_shape=jax.ShapeDtypeStruct((rows, cols), BF16),
        grid=(rows // tile,),
        in_specs=[
            pl.BlockSpec((tile, depth), lambda i: (i, 0)),
            pl.BlockSpec((tile, depth), lambda i: (i, 0)),
            pl.BlockSpec((depth, cols), lambda i: (0, 0)),
        ],
        out_specs=pl.BlockSpec((tile, cols), lambda i: (i, 0)),
        compiler_params=pltpu.CompilerParams(vmem_limit_bytes=14 * 1024 * 1024),
    )(hidden, cotangent, grads)


def tie(*values):
    return lax.optimization_barrier(values)


def hold_kernel(*refs):
    count = (len(refs) - 1) // 2
    for source, target in zip(refs[1 : 1 + count], refs[1 + count :]):
        target[...] = source[...]


def after(main, *held):
    tile = (16, HEAD_DIM)
    corners = [main[: tile[0], : tile[1]]]
    corners += [value[(0,) * (value.ndim - 2)][: tile[0], : tile[1]] for value in held]
    whole = pl.BlockSpec(memory_space=pltpu.VMEM)
    passed = pl.pallas_call(
        hold_kernel,
        out_shape=[jax.ShapeDtypeStruct(tile, value.dtype) for value in held],
        in_specs=[whole] * len(corners),
        out_specs=[whole] * len(held),
        compiler_params=pltpu.CompilerParams(vmem_limit_bytes=1024 * 1024),
        cost_estimate=pl.CostEstimate(flops=HOLD_FLOPS, bytes_accessed=HOLD_BYTES, transcendentals=0),
    )(*corners)
    return tuple(
        lax.dynamic_update_slice(value, tile.reshape((1,) * (value.ndim - 2) + tile.shape), (0,) * value.ndim)
        for value, tile in zip(held, passed)
    )


def rows(*pieces):
    return jnp.concatenate(pieces, axis=0)


def ordered(place, mine, other):
    return jnp.where(place == 0, rows(mine, other), rows(other, mine))


def gather_all(packed, block):
    yl_place, z_place = lax.axis_index("yl"), lax.axis_index("z")
    x_place, yh_place = lax.axis_index("x"), lax.axis_index("yh")
    n, cols = packed.shape
    side = cols // 2
    m, wide = block.shape
    wide //= 2
    weights = jnp.zeros((N_YL, N_Z, n, cols), BF16)
    features = jnp.zeros((N_X, N_YH * m, 2 * wide), BF16)

    def put_pair(weights, piece, step, row=0):
        piece = piece.reshape(N_YL, 1, -1, side)
        return lax.dynamic_update_slice(weights, piece, (0, (z_place + step) % N_Z, row, 0))

    def put_one(weights, piece, step, swapped, row=0):
        place = 1 - yl_place if swapped else yl_place
        return lax.dynamic_update_slice(
            weights, piece[None, None], (place, (z_place + step) % N_Z, row, side)
        )

    def put_x(features, piece, step, row=0):
        return lax.dynamic_update_slice(features, piece[None], ((x_place + step) % N_X, row, 0))

    first, second = packed[:, :side], packed[:, side:]
    other = shift(first, "yl", 1, N_YL)
    up, down = shift(second, "z", 1, N_Z), shift(second, "z", -1, N_Z)
    block_other = shift(block, "yh", 1, N_YH)

    pair = ordered(yl_place, first, other)
    weights = put_pair(weights, pair, 0)
    weights = put_one(weights, second, 0, False)
    weights = put_one(weights, up, -1, False)
    weights = put_one(weights, down, 1, False)
    ones = [up, down]
    up, down = tie(rows(pair, up), rows(pair, down))
    second, block = after(up, second, ordered(yh_place, block, block_other))
    up, down = shift(up, "z", 1, N_Z), shift(down, "z", -1, N_Z)
    other = shift(second, "yl", 1, N_YL)
    right, left = shift(block, "x", 1, N_X), shift(block, "x", -1, N_X)

    weights = put_pair(weights, up[: 2 * n], -1)
    weights = put_pair(weights, down[: 2 * n], 1)
    weights = put_one(weights, up[2 * n :], -2, False)
    weights = put_one(weights, down[2 * n :], 2, False)
    ones += [up[2 * n :], down[2 * n :]]
    up, down = tie(up, down)
    (others,) = after(up, rows(*ones))
    up, down = shift(up, "z", 1, N_Z), shift(down, "z", -1, N_Z)
    others = shift(others, "yl", 1, N_YL)

    weights = put_one(weights, other, 0, True)
    weights = put_pair(weights, up[: 2 * n], -2)
    weights = put_pair(weights, down[: 2 * n], 2)
    weights = put_one(weights, up[2 * n :], -3, False)
    weights = put_one(weights, down[2 * n :], 3, False)
    half = 2 * n + n // 2
    last = rows(up[2 * n :], down[2 * n :])
    up, down = tie(up[:half], rows(down[: 2 * n], down[half:]))
    last, far_right, far_left = after(up, last, right[:m], left[m:])
    up, down = shift(up, "z", 1, N_Z), shift(down, "z", -1, N_Z)
    last = shift(last, "yl", 1, N_YL)
    features = put_x(put_x(put_x(features, block, 0), right, -1), left, 1)
    right, left = shift(far_right, "x", 1, N_X), shift(far_left, "x", -1, N_X)

    for place, step in enumerate((-1, 1, -2, 2)):
        weights = put_one(weights, others[place * n : (place + 1) * n], step, True)
    weights = put_pair(weights, up[: 2 * n], -3)
    weights = put_pair(weights, down[: 2 * n], 3)
    other = rows(up[2 * n :], down[2 * n :])
    weights = put_one(weights, other, 4, False)
    upper = up[: 2 * n].reshape(N_YL, n, side)[:, : n // 2].reshape(n, side)
    lower = down[: 2 * n].reshape(N_YL, n, side)[:, n // 2 :].reshape(n, side)
    up, down = tie(upper, lower)
    (other,) = after(up, other)
    up, down = shift(up, "z", 1, N_Z), shift(down, "z", -1, N_Z)
    other = shift(other, "yl", 1, N_YL)

    weights = put_one(weights, last[:n], -3, True)
    weights = put_one(weights, last[n:], 3, True)
    weights = put_one(weights, other, 4, True)
    weights = put_pair(put_pair(weights, up, 4), down, 4, n // 2)
    features = put_x(put_x(features, right, 2), left, 2, m)
    features = features.reshape(N_X * N_YH * m, 2 * wide)
    return weights.reshape(N_YL * N_Z * n, cols), features[:, :wide], features[:, wide:]


def high_low(total):
    high = lax.reduce_precision(total, 8, 7)
    return jnp.concatenate([high.astype(BF16), (total - high).astype(BF16)], axis=-2)


def with_sums(values, sums):
    return jnp.concatenate([values.astype(BF16), high_low(sums)], axis=-2)


def apart(packed):
    sums = packed[..., -16:, :].astype(F32)
    return packed[..., :-16, :].astype(F32), sums[..., :8, :] + sums[..., 8:, :]


def fold_apart(*packed):
    values, sums = zip(*(apart(p) for p in packed))
    return sum(values), sum(sums)


def add(a, b):
    return (a.astype(F32) + b.astype(F32)).astype(BF16)


def reduce_back(grads, parts):
    yl_place, z_place = lax.axis_index("yl"), lax.axis_index("z")
    x_place, yh_place = lax.axis_index("x"), lax.axis_index("yh")
    _, _, n, cols = grads.shape
    side = cols // 2

    def pair(step):
        found = lax.dynamic_slice(grads, (0, (z_place + step) % N_Z, 0, 0), (N_YL, 1, n, side))
        return found.reshape(N_YL * n, side)

    def one(step, swapped):
        place = 1 - yl_place if swapped else yl_place
        found = lax.dynamic_slice(grads, (place, (z_place + step) % N_Z, 0, side), (1, 1, n, side))
        return found.reshape(n, side)

    def piece(values, step):
        return lax.dynamic_index_in_dim(values, (x_place + step) % N_X, 0, keepdims=False)

    def flat(values):
        return values.reshape(-1, values.shape[-1])

    def pick(values, place):
        return lax.dynamic_index_in_dim(values, place, 0, keepdims=False)

    def fold(mine, *arrived):
        return sum((a.astype(F32) for a in arrived), mine.astype(F32))

    def send_z(down, up):
        return tie(shift(down, "z", -1, N_Z), shift(up, "z", 1, N_Z))

    far = pair(4)
    down, up = send_z(far[:n], far[n:])
    far_other = shift(one(4, True), "yl", 1, N_YL)
    other = shift(rows(*(one(step, True) for step in (-3, 3, -2, 2))), "yl", 1, N_YL)
    packed = parts()
    down, up, far_other, packed = tie(down, up, far_other, packed)

    far = fold(one(4, False), far_other).astype(BF16)
    below, above = pair(-3), pair(3)
    down, up = tie(
        rows(add(below[:n], down), below[n:], far[: n // 2]),
        rows(above[:n], add(above[n:], up), far[n // 2 :]),
    )
    left, right = after(down, *piece(packed, 2))
    down, up = send_z(down, up)
    left, right = shift(left, "x", -1, N_X), shift(right, "x", 1, N_X)

    pad = jnp.zeros((n // 2, side), BF16)
    down, up = tie(
        rows(add(pair(-2), down[: 2 * n]), fold(one(-3, False), other[:n], rows(down[2 * n :], pad)).astype(BF16)),
        rows(add(pair(2), up[: 2 * n]), fold(one(3, False), other[n : 2 * n], rows(pad, up[2 * n :])).astype(BF16)),
    )
    mine_left, mine_right = piece(packed, -1), piece(packed, 1)
    other_next, left, right = after(
        down,
        rows(one(-1, True), one(1, True), one(0, True)),
        jnp.stack([with_sums(*fold_apart(mine_left[0], left)), mine_left[1]]),
        jnp.stack([mine_right[0], with_sums(*fold_apart(mine_right[1], right))]),
    )
    down, up = send_z(down, up)
    other_next = shift(other_next, "yl", 1, N_YL)
    left, right = shift(left, "x", -1, N_X), shift(right, "x", 1, N_X)

    down, up = tie(
        rows(add(pair(-1), down[: 2 * n]), fold(one(-2, False), other[2 * n : 3 * n], down[2 * n :]).astype(BF16)),
        rows(add(pair(1), up[: 2 * n]), fold(one(2, False), other[3 * n :], up[2 * n :]).astype(BF16)),
    )
    other = other_next
    values, sums = fold_apart(piece(packed, 0), left, right)
    (back,) = after(down, with_sums(pick(values, 1 - yh_place), pick(sums, 1 - yh_place)))
    down, up = send_z(down, up)
    back = shift(back, "yh", 1, N_YH)

    total = fold(pair(0), down[: 2 * n], up[: 2 * n]).reshape(N_YL, n, side)
    down, up = tie(
        fold(one(-1, False), other[:n], down[2 * n :]).astype(BF16),
        fold(one(1, False), other[n : 2 * n], up[2 * n :]).astype(BF16),
    )
    (sent,) = after(down, pick(total, 1 - yl_place).astype(BF16))
    down, up = send_z(down, up)
    first = pick(total, yl_place) + shift(sent, "yl", 1, N_YL).astype(F32)
    other_values, other_sums = apart(back)
    features = rows(pick(values, yh_place) + other_values, pick(sums, yh_place) + other_sums)
    second = fold(one(0, False), other[2 * n :], down, up)
    return jnp.concatenate([first, second], axis=1), features


def shards(tokens, w_query, w_key, w_value, w_out, cotangent):
    core = lax.axis_index("c")
    row_count, local_cols = tokens.shape
    width = w_query.shape[1]
    feat = w_query.shape[0]
    packed = jnp.concatenate([w_query, w_key, w_value, w_out.T], axis=1)
    tokens_t, cotangent_t = tokens.T, cotangent.T
    both = jnp.concatenate([tokens_t, cotangent_t], axis=1).reshape(
        local_cols // (N_C * feat), N_C, feat, 2 * row_count
    )
    kept = lax.dynamic_index_in_dim(both, core, 1, keepdims=False)
    sent = lax.dynamic_index_in_dim(both, 1 - core, 1, keepdims=False)
    other = shift(sent, "c", 1, N_C)
    other, packed = tie(other, packed)
    block = jnp.concatenate(
        [kept[..., :row_count], other[..., :row_count], kept[..., row_count:], other[..., row_count:]],
        axis=-1,
    ).reshape(local_cols // N_C, 4 * row_count)
    weights, tokens_c, cotangent_c = gather_all(packed, block)
    half_rows = tokens_c.shape[0]
    tokens_c = tokens_c.astype(F32)

    half_mean = jnp.mean(tokens_c, axis=0)
    half_square = jnp.sum((tokens_c - half_mean) ** 2, axis=0)
    half_stats = jnp.stack([half_mean, half_square])
    other_stats = shift(jnp.roll(half_stats, row_count, axis=1), "c", 1, N_C)
    mean = 0.5 * (half_stats[0] + other_stats[0])
    gap = half_stats[0] - other_stats[0]
    square = half_stats[1] + other_stats[1] + (0.5 * half_rows) * gap * gap
    spread = lax.rsqrt(square / (2 * half_rows) + EPS)
    normed = (tokens_c - mean) * spread
    hidden = normed.astype(BF16)

    def project(columns):
        return jnp.concatenate(
            [
                dot(hidden[:, columns], weights[:, : 3 * width], (0, 0)),
                dot(cotangent_c[:, columns], weights[:, 3 * width :], (0, 0)),
            ],
            axis=1,
        )

    from_other = shift(project(slice(row_count, None)), "c", 1, N_C)
    grads_mine = attention(project(slice(0, row_count)), from_other)
    grads = jnp.concatenate([grads_mine, shift(grads_mine, "c", 1, N_C)], axis=0)

    grad_scale = 1.0 / math.sqrt(row_count * N_YL * N_Z * N_C)
    weight_parts = weight_grads(hidden, cotangent_c, grads, 3 * width, grad_scale)
    hidden_part = dot(weights[:, : 3 * width], grads[:, : 3 * width], (1, 1))
    branch_part = dot(weights[:, 3 * width :], grads[:, 3 * width :], (1, 1))

    def parts():
        shape = (N_X, N_YH, local_cols // N_C, 2 * row_count)
        values = jnp.concatenate([hidden_part.reshape(shape), branch_part.reshape(shape)], axis=2)
        sums = jnp.stack([jnp.sum(hidden_part, axis=0), jnp.sum(hidden_part * normed, axis=0)])
        sums = jnp.broadcast_to(jnp.pad(sums, ((0, 6), (0, 0))), (N_X, N_YH, 8, 2 * row_count))
        return with_sums(values, sums)

    weight_sums, mine = reduce_back(weight_parts.reshape(N_YL, N_Z, feat, 4 * width), parts)
    weight_sums = weight_sums.astype(BF16)
    mine, other = mine[:, :row_count], shift(mine[:, row_count:], "c", 1, N_C)
    means = (mine[-8:-6] + other[-8:-6]) / (2 * half_rows)
    mine, other = (v[:local_cols].reshape(2, -1, 1, feat, row_count) for v in (mine, other))
    both = jnp.where(core == 0, jnp.concatenate([mine, other], 2), jnp.concatenate([other, mine], 2))
    hidden_sum, branch_sum = both.reshape(2, local_cols, row_count)
    own_normed = (tokens_t.astype(F32) - mean[:row_count]) * spread[:row_count]
    input_grad = spread[:row_count] * (hidden_sum - means[0] - own_normed * means[1])
    input_grad = (input_grad + cotangent_t.astype(F32)).astype(BF16).T
    output = (branch_sum + tokens_t.astype(F32)).astype(BF16).T
    return (
        output,
        input_grad,
        weight_sums[:, :width],
        weight_sums[:, width : 2 * width],
        weight_sums[:, 2 * width : 3 * width],
        weight_sums[:, 3 * width :].T,
    )


def solution(mesh):
    split = Mesh(
        mesh.devices.reshape(N_YL, N_Z, N_C, N_X, N_YH), ("yl", "z", "c", "x", "yh")
    )
    dp, mp = ("yl", "z", "c"), ("x", "yh")
    placed = (P(dp, mp),) * 4 + (P(mp, dp), P(dp, mp))
    return jax.shard_map(
        shards,
        mesh=split,
        in_specs=placed,
        out_specs=(P(dp, mp),) * 5 + (P(mp, dp),),
        check_vma=False,
    )
```

```python
import math

import jax
import jax.numpy as jnp
from jax import lax
from jax.experimental import pallas as pl
from jax.experimental.pallas import tpu as pltpu
from jax.sharding import Mesh
from jax.sharding import PartitionSpec as P

HEAD_DIM = 128
IMG_TOK = 64
EPS = 1e-06
BF16 = jnp.bfloat16
F32 = jnp.float32
N_YL, N_Z, N_C, N_X, N_YH = 2, 8, 2, 4, 2
HOLD_FLOPS, HOLD_BYTES = 12_000_000_000, 40_000_000


def shift(value, axis, step, size):
    return lax.ppermute(value, axis, [(i, (i + step) % size) for i in range(size)])


def dot(a, b, contract):
    return lax.dot_general(a, b, ((contract[:1], contract[1:]), ((), ())), preferred_element_type=F32)


def norm_parts(raw):
    center = raw - jnp.mean(raw, axis=-1, keepdims=True)
    spread = lax.rsqrt(jnp.mean(center * center, axis=-1, keepdims=True) + EPS)
    return center * spread, spread


def norm_back(grad, normed, spread):
    first = jnp.mean(grad, axis=-1, keepdims=True)
    second = jnp.mean(grad * normed, axis=-1, keepdims=True)
    return spread * (grad - first - normed * second)


def attention_kernel(mine_ref, other_ref, grads_ref):
    rows, cols = mine_ref.shape
    width = cols // 4
    image = lax.broadcasted_iota(jnp.int32, (rows, rows), 0) // IMG_TOK
    same = image == lax.broadcasted_iota(jnp.int32, (rows, rows), 1) // IMG_TOK
    scale = 1.0 / math.sqrt(HEAD_DIM)
    for head in range(width // HEAD_DIM):
        spans = [pl.ds(part * width + head * HEAD_DIM, HEAD_DIM) for part in range(4)]
        query_raw, key_raw, value_raw, attended_grad = (
            mine_ref[:, span] + other_ref[:, span].astype(F32) for span in spans
        )
        query_normed, query_spread = norm_parts(query_raw)
        key_normed, key_spread = norm_parts(key_raw)
        query, key, value = query_normed.astype(BF16), key_normed.astype(BF16), value_raw.astype(BF16)
        attended_grad = attended_grad.astype(BF16)
        weights = jnp.where(same, jnp.exp(dot(query, key, (1, 1)) * scale), 0.0)
        exact = weights / jnp.sum(weights, axis=-1, keepdims=True)
        probability = exact.astype(BF16)
        attended = dot(probability, value, (1, 0))
        value_grad = dot(probability, attended_grad, (0, 0))
        probability_grad = dot(attended_grad, value, (1, 1)).astype(BF16).astype(F32)
        inner = jnp.sum(probability_grad * exact, axis=-1, keepdims=True)
        scores_grad = (exact * (probability_grad - inner) * scale).astype(BF16)
        query_grad = dot(scores_grad, key, (1, 0)).astype(BF16).astype(F32)
        key_grad = dot(scores_grad, query, (0, 0)).astype(BF16).astype(F32)
        grads_ref[:, spans[0]] = norm_back(query_grad, query_normed, query_spread).astype(BF16)
        grads_ref[:, spans[1]] = norm_back(key_grad, key_normed, key_spread).astype(BF16)
        grads_ref[:, spans[2]] = value_grad.astype(BF16)
        grads_ref[:, spans[3]] = attended.astype(BF16)


def attention(mine, other):
    whole = pl.BlockSpec(memory_space=pltpu.VMEM)
    return pl.pallas_call(
        attention_kernel,
        out_shape=jax.ShapeDtypeStruct(mine.shape, BF16),
        in_specs=[whole, whole],
        out_specs=whole,
        compiler_params=pltpu.CompilerParams(vmem_limit_bytes=14 * 1024 * 1024),
    )(mine, other)


def weight_kernel(hidden_ref, cotangent_ref, grads_ref, out_ref, *, split, scale):
    first = dot(hidden_ref[...], grads_ref[:, :split], (1, 0))
    out_ref[:, :split] = (first * scale).astype(BF16)
    second = dot(cotangent_ref[...], grads_ref[:, split:], (1, 0))
    out_ref[:, split:] = (second * scale).astype(BF16)


def weight_grads(hidden, cotangent, grads, split, scale):
    rows, depth = hidden.shape
    cols = grads.shape[1]
    tile = rows // 4
    return pl.pallas_call(
        lambda *refs: weight_kernel(*refs, split=split, scale=scale),
        out_shape=jax.ShapeDtypeStruct((rows, cols), BF16),
        grid=(rows // tile,),
        in_specs=[
            pl.BlockSpec((tile, depth), lambda i: (i, 0)),
            pl.BlockSpec((tile, depth), lambda i: (i, 0)),
            pl.BlockSpec((depth, cols), lambda i: (0, 0)),
        ],
        out_specs=pl.BlockSpec((tile, cols), lambda i: (i, 0)),
        compiler_params=pltpu.CompilerParams(vmem_limit_bytes=14 * 1024 * 1024),
    )(hidden, cotangent, grads)


def tie(*values):
    return lax.optimization_barrier(values)


def hold_kernel(*refs):
    count = (len(refs) - 1) // 2
    for source, target in zip(refs[1 : 1 + count], refs[1 + count :]):
        target[...] = source[...]


def after(main, *held):
    tile = (16, HEAD_DIM)
    corners = [main[: tile[0], : tile[1]]]
    corners += [value[(0,) * (value.ndim - 2)][: tile[0], : tile[1]] for value in held]
    whole = pl.BlockSpec(memory_space=pltpu.VMEM)
    passed = pl.pallas_call(
        hold_kernel,
        out_shape=[jax.ShapeDtypeStruct(tile, value.dtype) for value in held],
        in_specs=[whole] * len(corners),
        out_specs=[whole] * len(held),
        compiler_params=pltpu.CompilerParams(vmem_limit_bytes=1024 * 1024),
        cost_estimate=pl.CostEstimate(flops=HOLD_FLOPS, bytes_accessed=HOLD_BYTES, transcendentals=0),
    )(*corners)
    return tuple(
        lax.dynamic_update_slice(value, tile.reshape((1,) * (value.ndim - 2) + tile.shape), (0,) * value.ndim)
        for value, tile in zip(held, passed)
    )


def rows(*pieces):
    return jnp.concatenate(pieces, axis=0)


def ordered(place, mine, other):
    return jnp.where(place == 0, rows(mine, other), rows(other, mine))


def gather_all(packed, block):
    yl_place, z_place = lax.axis_index("yl"), lax.axis_index("z")
    x_place, yh_place = lax.axis_index("x"), lax.axis_index("yh")
    n, cols = packed.shape
    side = cols // 2
    m, wide = block.shape
    wide //= 2
    weights = jnp.zeros((N_YL, N_Z, n, cols), BF16)
    features = jnp.zeros((N_X, N_YH * m, 2 * wide), BF16)

    def put_pair(weights, piece, step, row=0):
        piece = piece.reshape(N_YL, 1, -1, side)
        return lax.dynamic_update_slice(weights, piece, (0, (z_place + step) % N_Z, row, 0))

    def put_one(weights, piece, step, swapped, row=0):
        place = 1 - yl_place if swapped else yl_place
        return lax.dynamic_update_slice(
            weights, piece[None, None], (place, (z_place + step) % N_Z, row, side)
        )

    def put_x(features, piece, step, row=0):
        return lax.dynamic_update_slice(features, piece[None], ((x_place + step) % N_X, row, 0))

    first, second = packed[:, :side], packed[:, side:]
    other = shift(first, "yl", 1, N_YL)
    up, down = shift(second, "z", 1, N_Z), shift(second, "z", -1, N_Z)
    block_other = shift(block, "yh", 1, N_YH)

    pair = ordered(yl_place, first, other)
    weights = put_pair(weights, pair, 0)
    weights = put_one(weights, second, 0, False)
    weights = put_one(weights, up, -1, False)
    weights = put_one(weights, down, 1, False)
    ones = [up, down]
    up, down = tie(rows(pair, up), rows(pair, down))
    second, block = after(up, second, ordered(yh_place, block, block_other))
    up, down = shift(up, "z", 1, N_Z), shift(down, "z", -1, N_Z)
    other = shift(second, "yl", 1, N_YL)
    right, left = shift(block, "x", 1, N_X), shift(block, "x", -1, N_X)

    weights = put_pair(weights, up[: 2 * n], -1)
    weights = put_pair(weights, down[: 2 * n], 1)
    weights = put_one(weights, up[2 * n :], -2, False)
    weights = put_one(weights, down[2 * n :], 2, False)
    ones += [up[2 * n :], down[2 * n :]]
    up, down = tie(up, down)
    (others,) = after(up, rows(*ones))
    up, down = shift(up, "z", 1, N_Z), shift(down, "z", -1, N_Z)
    others = shift(others, "yl", 1, N_YL)

    weights = put_one(weights, other, 0, True)
    weights = put_pair(weights, up[: 2 * n], -2)
    weights = put_pair(weights, down[: 2 * n], 2)
    weights = put_one(weights, up[2 * n :], -3, False)
    weights = put_one(weights, down[2 * n :], 3, False)
    half = 2 * n + n // 2
    last = rows(up[2 * n :], down[2 * n :])
    up, down = tie(up[:half], rows(down[: 2 * n], down[half:]))
    last, far_right, far_left = after(up, last, right[:m], left[m:])
    up, down = shift(up, "z", 1, N_Z), shift(down, "z", -1, N_Z)
    last = shift(last, "yl", 1, N_YL)
    features = put_x(put_x(put_x(features, block, 0), right, -1), left, 1)
    right, left = shift(far_right, "x", 1, N_X), shift(far_left, "x", -1, N_X)

    for place, step in enumerate((-1, 1, -2, 2)):
        weights = put_one(weights, others[place * n : (place + 1) * n], step, True)
    weights = put_pair(weights, up[: 2 * n], -3)
    weights = put_pair(weights, down[: 2 * n], 3)
    other = rows(up[2 * n :], down[2 * n :])
    weights = put_one(weights, other, 4, False)
    upper = up[: 2 * n].reshape(N_YL, n, side)[:, : n // 2].reshape(n, side)
    lower = down[: 2 * n].reshape(N_YL, n, side)[:, n // 2 :].reshape(n, side)
    up, down = tie(upper, lower)
    (other,) = after(up, other)
    up, down = shift(up, "z", 1, N_Z), shift(down, "z", -1, N_Z)
    other = shift(other, "yl", 1, N_YL)

    weights = put_one(weights, last[:n], -3, True)
    weights = put_one(weights, last[n:], 3, True)
    weights = put_one(weights, other, 4, True)
    weights = put_pair(put_pair(weights, up, 4), down, 4, n // 2)
    features = put_x(put_x(features, right, 2), left, 2, m)
    features = features.reshape(N_X * N_YH * m, 2 * wide)
    return weights.reshape(N_YL * N_Z * n, cols), features[:, :wide], features[:, wide:]


def high_low(total):
    high = lax.reduce_precision(total, 8, 7)
    return jnp.concatenate([high.astype(BF16), (total - high).astype(BF16)], axis=-2)


def with_sums(values, sums):
    return jnp.concatenate([values.astype(BF16), high_low(sums)], axis=-2)


def apart(packed):
    sums = packed[..., -16:, :].astype(F32)
    return packed[..., :-16, :].astype(F32), sums[..., :8, :] + sums[..., 8:, :]


def fold_apart(*packed):
    values, sums = zip(*(apart(p) for p in packed))
    return sum(values), sum(sums)


def add(a, b):
    return (a.astype(F32) + b.astype(F32)).astype(BF16)


def reduce_back(grads, parts):
    yl_place, z_place = lax.axis_index("yl"), lax.axis_index("z")
    x_place, yh_place = lax.axis_index("x"), lax.axis_index("yh")
    _, _, n, cols = grads.shape
    side = cols // 2

    def pair(step):
        found = lax.dynamic_slice(grads, (0, (z_place + step) % N_Z, 0, 0), (N_YL, 1, n, side))
        return found.reshape(N_YL * n, side)

    def one(step, swapped):
        place = 1 - yl_place if swapped else yl_place
        found = lax.dynamic_slice(grads, (place, (z_place + step) % N_Z, 0, side), (1, 1, n, side))
        return found.reshape(n, side)

    def piece(values, step):
        return lax.dynamic_index_in_dim(values, (x_place + step) % N_X, 0, keepdims=False)

    def flat(values):
        return values.reshape(-1, values.shape[-1])

    def pick(values, place):
        return lax.dynamic_index_in_dim(values, place, 0, keepdims=False)

    def fold(mine, *arrived):
        return sum((a.astype(F32) for a in arrived), mine.astype(F32))

    def send_z(down, up):
        return tie(shift(down, "z", -1, N_Z), shift(up, "z", 1, N_Z))

    far = pair(4)
    down, up = send_z(far[:n], far[n:])
    far_other = shift(one(4, True), "yl", 1, N_YL)
    other = shift(rows(*(one(step, True) for step in (-3, 3, -2, 2))), "yl", 1, N_YL)
    packed = parts()
    down, up, far_other, packed = tie(down, up, far_other, packed)

    far = fold(one(4, False), far_other).astype(BF16)
    below, above = pair(-3), pair(3)
    down, up = tie(
        rows(add(below[:n], down), below[n:], far[: n // 2]),
        rows(above[:n], add(above[n:], up), far[n // 2 :]),
    )
    left, right = after(down, *piece(packed, 2))
    down, up = send_z(down, up)
    left, right = shift(left, "x", -1, N_X), shift(right, "x", 1, N_X)

    pad = jnp.zeros((n // 2, side), BF16)
    down, up = tie(
        rows(add(pair(-2), down[: 2 * n]), fold(one(-3, False), other[:n], rows(down[2 * n :], pad)).astype(BF16)),
        rows(add(pair(2), up[: 2 * n]), fold(one(3, False), other[n : 2 * n], rows(pad, up[2 * n :])).astype(BF16)),
    )
    mine_left, mine_right = piece(packed, -1), piece(packed, 1)
    other_next, left, right = after(
        down,
        rows(one(-1, True), one(1, True), one(0, True)),
        jnp.stack([with_sums(*fold_apart(mine_left[0], left)), mine_left[1]]),
        jnp.stack([mine_right[0], with_sums(*fold_apart(mine_right[1], right))]),
    )
    down, up = send_z(down, up)
    other_next = shift(other_next, "yl", 1, N_YL)
    left, right = shift(left, "x", -1, N_X), shift(right, "x", 1, N_X)

    down, up = tie(
        rows(add(pair(-1), down[: 2 * n]), fold(one(-2, False), other[2 * n : 3 * n], down[2 * n :]).astype(BF16)),
        rows(add(pair(1), up[: 2 * n]), fold(one(2, False), other[3 * n :], up[2 * n :]).astype(BF16)),
    )
    other = other_next
    values, sums = fold_apart(piece(packed, 0), left, right)
    (back,) = after(down, with_sums(pick(values, 1 - yh_place), pick(sums, 1 - yh_place)))
    down, up = send_z(down, up)
    back = shift(back, "yh", 1, N_YH)

    total = fold(pair(0), down[: 2 * n], up[: 2 * n]).reshape(N_YL, n, side)
    down, up = tie(
        fold(one(-1, False), other[:n], down[2 * n :]).astype(BF16),
        fold(one(1, False), other[n : 2 * n], up[2 * n :]).astype(BF16),
    )
    (sent,) = after(down, pick(total, 1 - yl_place).astype(BF16))
    down, up = send_z(down, up)
    first = pick(total, yl_place) + shift(sent, "yl", 1, N_YL).astype(F32)
    other_values, other_sums = apart(back)
    features = rows(pick(values, yh_place) + other_values, pick(sums, yh_place) + other_sums)
    second = fold(one(0, False), other[2 * n :], down, up)
    return jnp.concatenate([first, second], axis=1), features


def shards(tokens, w_query, w_key, w_value, w_out, cotangent):
    core = lax.axis_index("c")
    row_count, local_cols = tokens.shape
    width = w_query.shape[1]
    feat = w_query.shape[0]
    packed = jnp.concatenate([w_query, w_key, w_value, w_out.T], axis=1)
    tokens_t, cotangent_t = tokens.T, cotangent.T
    both = jnp.concatenate([tokens_t, cotangent_t], axis=1).reshape(
        local_cols // (N_C * feat), N_C, feat, 2 * row_count
    )
    kept = lax.dynamic_index_in_dim(both, core, 1, keepdims=False)
    sent = lax.dynamic_index_in_dim(both, 1 - core, 1, keepdims=False)
    other = shift(sent, "c", 1, N_C)
    other, packed = tie(other, packed)
    block = jnp.concatenate(
        [kept[..., :row_count], other[..., :row_count], kept[..., row_count:], other[..., row_count:]],
        axis=-1,
    ).reshape(local_cols // N_C, 4 * row_count)
    weights, tokens_c, cotangent_c = gather_all(packed, block)
    half_rows = tokens_c.shape[0]
    tokens_c = tokens_c.astype(F32)

    half_mean = jnp.mean(tokens_c, axis=0)
    half_square = jnp.sum((tokens_c - half_mean) ** 2, axis=0)
    half_stats = jnp.stack([half_mean, half_square])
    other_stats = shift(jnp.roll(half_stats, row_count, axis=1), "c", 1, N_C)
    mean = 0.5 * (half_stats[0] + other_stats[0])
    gap = half_stats[0] - other_stats[0]
    square = half_stats[1] + other_stats[1] + (0.5 * half_rows) * gap * gap
    spread = lax.rsqrt(square / (2 * half_rows) + EPS)
    normed = (tokens_c - mean) * spread
    hidden = normed.astype(BF16)

    def project(columns):
        return jnp.concatenate(
            [
                dot(hidden[:, columns], weights[:, : 3 * width], (0, 0)),
                dot(cotangent_c[:, columns], weights[:, 3 * width :], (0, 0)),
            ],
            axis=1,
        )

    from_other = shift(project(slice(row_count, None)).astype(BF16), "c", 1, N_C)
    grads_mine = attention(project(slice(0, row_count)), from_other)
    grads = jnp.concatenate([grads_mine, shift(grads_mine, "c", 1, N_C)], axis=0)

    grad_scale = 1.0 / math.sqrt(row_count * N_YL * N_Z * N_C)
    weight_parts = weight_grads(hidden, cotangent_c, grads, 3 * width, grad_scale)
    hidden_part = dot(weights[:, : 3 * width], grads[:, : 3 * width], (1, 1))
    branch_part = dot(weights[:, 3 * width :], grads[:, 3 * width :], (1, 1))

    def parts():
        shape = (N_X, N_YH, local_cols // N_C, 2 * row_count)
        values = jnp.concatenate([hidden_part.reshape(shape), branch_part.reshape(shape)], axis=2)
        sums = jnp.stack([jnp.sum(hidden_part, axis=0), jnp.sum(hidden_part * normed, axis=0)])
        sums = jnp.broadcast_to(jnp.pad(sums, ((0, 6), (0, 0))), (N_X, N_YH, 8, 2 * row_count))
        return with_sums(values, sums)

    weight_sums, mine = reduce_back(weight_parts.reshape(N_YL, N_Z, feat, 4 * width), parts)
    weight_sums = weight_sums.astype(BF16)
    mine, other = mine[:, :row_count], shift(mine[:, row_count:], "c", 1, N_C)
    means = (mine[-8:-6] + other[-8:-6]) / (2 * half_rows)
    mine, other = (v[:local_cols].reshape(2, -1, 1, feat, row_count) for v in (mine, other))
    both = jnp.where(core == 0, jnp.concatenate([mine, other], 2), jnp.concatenate([other, mine], 2))
    hidden_sum, branch_sum = both.reshape(2, local_cols, row_count)
    own_normed = (tokens_t.astype(F32) - mean[:row_count]) * spread[:row_count]
    input_grad = spread[:row_count] * (hidden_sum - means[0] - own_normed * means[1])
    input_grad = (input_grad + cotangent_t.astype(F32)).astype(BF16).T
    output = (branch_sum + tokens_t.astype(F32)).astype(BF16).T
    return (
        output,
        input_grad,
        weight_sums[:, :width],
        weight_sums[:, width : 2 * width],
        weight_sums[:, 2 * width : 3 * width],
        weight_sums[:, 3 * width :].T,
    )


def solution(mesh):
    split = Mesh(
        mesh.devices.reshape(N_YL, N_Z, N_C, N_X, N_YH), ("yl", "z", "c", "x", "yh")
    )
    dp, mp = ("yl", "z", "c"), ("x", "yh")
    placed = (P(dp, mp),) * 4 + (P(mp, dp), P(dp, mp))
    return jax.shard_map(
        shards,
        mesh=split,
        in_specs=placed,
        out_specs=(P(dp, mp),) * 5 + (P(mp, dp),),
        check_vma=False,
    )
```
